32 devices in a mesh: seq: 32 (over z, y, x, core).
Axes of the slice: x: 2, y: 2, z: 4, core: 2. Of those that a mesh axis runs over, the one named last changes fastest.
Arguments:
- queries: bfloat16 [4096, 2048], P('seq'), may hold values from -4.5 to 4.5
- keys: bfloat16 [4096, 512], P('seq'), may hold values from -4.5 to 4.5
- values: bfloat16 [4096, 512], P('seq'), may hold values from -6 to 6
- selected: int32 [32, 4, 32], P('seq'), may hold values from 0 to 127, as said below
Outputs:
- attended: bfloat16 [4096, 2048], P('seq')
The draws below stay inside these ranges and needn't reach their ends.
Inputs may be any that keep to these rules, and one draw needn't show every extreme that they name: Each row selected[b, g] holds 32 distinct positions.
All inputs are finite; a program needn't handle non-finite values.
Results may differ from the reference program's by a relative error of at most 0.005.
Values may be sent and summed in bfloat16 or wider, within the bound.
A program may use at most 192 MiB of HBM per device.

```python
import math
import jax
import jax.numpy as jnp
from jax import lax

HD = 128
QH = 16
KVH = 4
PASS = 32
TOK_DEV = 128
BLOCKS = 32
TOKENS = 4096


def draw_queries(key, part):
    key = jax.random.fold_in(key, 11)
    drawn = jnp.clip(jax.random.normal(key, (TOKENS, QH, HD), jnp.float32), -4.5, 4.5)
    return drawn.reshape(TOKENS, QH * HD).astype(jnp.bfloat16)


def draw_keys(key, part):
    key = jax.random.fold_in(key, 12)
    drawn = jnp.clip(jax.random.normal(key, (TOKENS, KVH, HD), jnp.float32), -4.5, 4.5)
    return drawn.reshape(TOKENS, KVH * HD).astype(jnp.bfloat16)


def draw_selected(key, part):
    key = jax.random.fold_in(key, 7)
    random_bits = jax.random.randint(key, (BLOCKS * KVH, TOK_DEV), 0, 4096)
    column = jnp.arange(TOK_DEV, dtype=jnp.int32)[None, :]
    row_index = jnp.arange(BLOCKS * KVH, dtype=jnp.int32)[:, None]
    ranking = random_bits * TOK_DEV + column
    ranking = jnp.where((row_index == 0) & (column == 0), -2, ranking)
    ranking = jnp.where((row_index == 0) & (column == TOK_DEV - 1), -1, ranking)
    chosen = jnp.argsort(ranking, axis=1, stable=True)[:, :PASS]
    return chosen.reshape(BLOCKS, KVH, PASS).astype(jnp.int32)


def steps_of(rng, extent, cuts, low, top_value):
    gain = 1.0
    for dim, shards_of in cuts:
        draws = jax.random.uniform(jax.random.fold_in(jax.random.fold_in(rng, 6), dim), (shards_of,), jnp.float32, low / len(cuts), top_value / len(cuts))
        gain = gain * jnp.repeat(jnp.exp(draws), extent[dim] // shards_of).reshape((-1,) + (1,) * (len(extent) - 1 - dim))
    return gain


def bell_draw(key, shape, spread, reach, cuts=(), kind=jnp.bfloat16):
    values = jax.random.normal(key, shape, jnp.float32) * spread
    if len(cuts) > 0:
        values = steps_of(key, shape, cuts, -0.22, 0.18) * values
    return jnp.clip(values, min=-reach, max=reach).astype(kind)


def setup_inputs(seed: int = 0) -> dict:
    arg_keys = jax.random.split(jax.random.key(seed), 5)
    return {
        "queries": draw_queries(jax.random.fold_in(arg_keys[4], 71), 0),
        "keys": draw_keys(jax.random.fold_in(arg_keys[4], 71), 0),
        "values": bell_draw(arg_keys[2], (TOKENS, KVH * HD), 1.0, 6.0, ((0, 32),)),
        "selected": draw_selected(jax.random.fold_in(arg_keys[4], 71), 0),
    }


def reference(queries, keys, values, selected):
    group_size = QH // KVH
    score_scale = 1.0 / math.sqrt(HD)
    query_all = queries.reshape(BLOCKS, TOK_DEV, KVH, group_size, HD)
    key_all = keys.reshape(BLOCKS, TOK_DEV, KVH, HD).astype(jnp.float32)
    value_all = values.reshape(BLOCKS, TOK_DEV, KVH, HD).astype(jnp.float32)
    one_hot = (selected[:, :, :, None] == jnp.arange(TOK_DEV, dtype=jnp.int32)).astype(jnp.float32)
    pass_keys = jnp.einsum('bgpt,btgd->bpgd', one_hot, key_all).reshape(BLOCKS * PASS, KVH, HD)
    pass_values = jnp.einsum('bgpt,btgd->bpgd', one_hot, value_all).reshape(BLOCKS * PASS, KVH, HD)
    source = jnp.arange(BLOCKS * PASS, dtype=jnp.int32) // PASS
    position = jnp.arange(TOK_DEV, dtype=jnp.int32)
    causal = position[None, :] <= position[:, None]

    def attend_block(block):
        query_here = query_all[block].astype(jnp.float32)
        key_set = jnp.concatenate([key_all[block], key_all[0], pass_keys], axis=0)
        value_set = jnp.concatenate([value_all[block], value_all[0], pass_values], axis=0)
        anchor_seen = jnp.broadcast_to(block > 0, (TOK_DEV, TOK_DEV))
        passing_seen = jnp.broadcast_to(((source >= 1) & (source < block))[None, :], (TOK_DEV, BLOCKS * PASS))
        visible = jnp.concatenate([causal, anchor_seen, passing_seen], axis=1)
        scores = jnp.einsum('tgjd,sgd->gjts', query_here, key_set) * score_scale
        scores = jnp.where(visible, scores, -jnp.inf)
        top = lax.optimization_barrier(jnp.max(scores, axis=-1, keepdims=True))
        weights = jnp.where(visible, jnp.exp(scores - top), 0.0)
        totals = lax.optimization_barrier(jnp.sum(weights, axis=-1))
        rounded = lax.optimization_barrier(weights.astype(jnp.bfloat16)).astype(jnp.float32)
        mixed = jnp.einsum('gjts,sgd->tgjd', rounded, value_set)
        mixed = mixed / jnp.transpose(totals, (2, 0, 1))[..., None]
        return mixed.reshape(TOK_DEV, QH * HD).astype(jnp.bfloat16)
    blocks_out = lax.map(attend_block, jnp.arange(BLOCKS, dtype=jnp.int32))
    return blocks_out.reshape(BLOCKS * TOK_DEV, QH * HD)
```

```python
import functools
import math

import jax
import jax.numpy as jnp
from jax import lax
from jax.experimental import pallas as pl
from jax.experimental.pallas import tpu as pltpu
from jax.sharding import PartitionSpec as P

HD = 128
QH = 16
KVH = 4
PASS = 32
TOK_DEV = 128
GROUP = QH // KVH
PLANE = 8
LOG2_SCALE = math.log2(math.e) / math.sqrt(HD)
very_negative = -1e30
MESH = pl.DeviceIdType.MESH


def dot_t(a, b):
    return lax.dot_general(a, b, (((1,), (1,)), ((), ())), preferred_element_type=jnp.float32)


def dot(a, b):
    return lax.dot_general(a, b, (((1,), (0,)), ((), ())), preferred_element_type=jnp.float32)


def kernel(n, q_ref, k_ref, v_ref, sel_ref, o_ref, buf, anchor, acc, best, tot,
           packet_recv, anchor_recv, packet_send, anchor_send, z_send, anchor_z_send, scatter_send):
    planes = n // PLANE
    me = lax.axis_index("seq")
    plane = me // PLANE
    r = me % PLANE
    core = r % 2
    x = (r // 2) % 2
    y = r // 4
    near_x = r + 2 - 4 * x
    near_y = r + 4 - 8 * y
    first = near_x * (1 - core) + near_y * core
    second = near_y * (1 - core) + near_x * core
    across = near_x + near_y - r
    to_sib = 1 - 2 * core
    home = plane * PLANE

    barrier = pltpu.get_barrier_semaphore()

    def greet_plane(i, carry):
        pl.semaphore_signal(barrier, inc=1, device_id=(home + (r + i) % PLANE,), device_id_type=MESH)
        return carry

    def greet_line(i, carry):
        pl.semaphore_signal(barrier, inc=1, device_id=(((plane + i) % planes) * PLANE + r,), device_id_type=MESH)
        return carry

    lax.fori_loop(1, PLANE, greet_plane, 0)
    lax.fori_loop(1, planes, greet_line, 0)

    lane = lax.broadcasted_iota(jnp.int32, (PASS, PASS), 1)
    row = lax.broadcasted_iota(jnp.int32, (PASS, PASS), 0)
    token = lax.broadcasted_iota(jnp.int32, (PASS, TOK_DEV), 1).astype(jnp.float32)
    for g in range(KVH):
        sel = sel_ref[0, g:g + 1, :].astype(jnp.float32)
        column = jnp.sum(jnp.where(lane == row, sel, 0.0), axis=1, keepdims=True)
        one_hot = jnp.where(token == column, 1.0, 0.0).astype(jnp.bfloat16)
        cols = slice(g * HD, (g + 1) * HD)
        buf[me, g] = dot(one_hot, k_ref[:, cols]).astype(jnp.bfloat16)
        buf[me, KVH + g] = dot(one_hot, v_ref[:, cols]).astype(jnp.bfloat16)

    pl.semaphore_wait(barrier, PLANE - 1 + planes - 1)

    def remote(ref, send_sem, recv_sem, device):
        return pltpu.make_async_remote_copy(
            src_ref=ref, dst_ref=ref, send_sem=send_sem, recv_sem=recv_sem,
            device_id=(device,), device_id_type=MESH)

    class Stage:
        def __init__(self, piece, recv, send):
            self.piece, self.recv, self.send = piece, recv, send

        def arrived(self, rr):
            remote(self.piece(rr), self.send(0), self.recv(rr), home + first).wait_recv()

        def push(self, rr, target, i):
            remote(self.piece(rr), self.send(i), self.recv(rr), home + target).start()

        def issue(self):
            self.push(r, first, 0)
            self.push(r, second, 1)
            self.push(r, r + to_sib, 2)

        def relay(self):
            self.arrived(first)
            self.push(first, second, 3)
            self.push(first, r + to_sib, 4)
            self.arrived(second)
            self.push(second, r + to_sib, 5)

        def finish(self):
            self.arrived(across)
            self.push(across, r + to_sib, 6)

        def gathered(self):
            for rr in (r, first, second, across):
                self.arrived(rr + to_sib)

        def sent(self):
            for i in range(7):
                remote(self.piece(r), self.send(i), self.recv(r), home + first).wait_send()

    def packet(q):
        return Stage(lambda rr: buf.at[q * PLANE + rr], lambda rr: packet_recv.at[q * PLANE + rr],
                     lambda i: packet_send.at[q, i])

    block0 = Stage(lambda rr: anchor.at[rr], lambda rr: anchor_recv.at[rr], lambda i: anchor_send.at[i])

    def send_line(ref, sems, recv_sem):
        def one(other, carry):
            remote(ref, sems.at[other], recv_sem, other * PLANE + r).start()
            return carry

        lax.fori_loop(plane + 1, planes, one, 0)

    def sent_line(ref, sems, recv_sem):
        def one(other, carry):
            remote(ref, sems.at[other], recv_sem, other * PLANE + r).wait_send()
            return carry

        lax.fori_loop(plane + 1, planes, one, 0)

    def scatter(j):
        source = k_ref if j < KVH else v_ref
        cols = pl.ds((j % KVH) * HD, HD)
        return pltpu.make_async_remote_copy(
            src_ref=source.at[:, cols], dst_ref=anchor.at[j], send_sem=scatter_send.at[j],
            recv_sem=anchor_recv.at[j], device_id=(j,), device_id_type=MESH)

    @pl.when(me == 0)
    def _():
        for j in range(1, PLANE):
            scatter(j).start()
        anchor[0] = k_ref[:, :HD]

    send_line(buf.at[me], z_send, packet_recv.at[me])
    packet(plane).issue()

    def head_queries(g):
        return jnp.concatenate(
            [q_ref[:, pl.ds(pl.multiple_of((g * GROUP + j) * HD, HD), HD)] for j in range(GROUP)], axis=0)

    def lane_tiles(w):
        return [w[:, i * HD:(i + 1) * HD] for i in range(w.shape[1] // HD)]

    rows = GROUP * TOK_DEV

    def own(g, carry):
        cols = pl.ds(pl.multiple_of(g * HD, HD), HD)
        s = dot_t(head_queries(g), k_ref[:, cols]) * LOG2_SCALE
        position = lax.broadcasted_iota(jnp.int32, (rows, TOK_DEV), 0) % TOK_DEV
        key_at = lax.broadcasted_iota(jnp.int32, (rows, TOK_DEV), 1)
        s = jnp.where(key_at <= position, s, very_negative)
        top = jnp.broadcast_to(jnp.max(s, axis=1, keepdims=True), (rows, HD))
        w = jnp.exp2(s - top)
        best[g] = top
        tot[g] = w
        acc[g] = dot(w.astype(jnp.bfloat16), v_ref[:, cols])
        return carry

    def update(g, key_rows, value_rows, bias):
        s = dot_t(head_queries(g), key_rows) * LOG2_SCALE
        if bias is not None:
            s = s + bias
        tiles = lane_tiles(s)
        old = best[g]
        top = jnp.max(functools.reduce(jnp.maximum, tiles), axis=1, keepdims=True)
        top = jnp.maximum(old, top)
        w = [jnp.exp2(t - top) for t in tiles]
        rescale = jnp.exp2(old - top)
        best[g] = top
        tot[g] = tot[g] * rescale + functools.reduce(jnp.add, w)
        w = jnp.concatenate([t.astype(jnp.bfloat16) for t in w], axis=1)
        acc[g] = acc[g] * rescale + dot(w, value_rows)

    def use_packets(q):
        source = q * PLANE + lax.broadcasted_iota(jnp.int32, (1, PLANE * PASS), 1) // PASS
        bias = jnp.where((source >= 1) & (source < me), 0.0, very_negative)
        at = pl.ds(q * PLANE, PLANE)

        def one(g, carry):
            update(g, buf[at, g].reshape(PLANE * PASS, HD), buf[at, KVH + g].reshape(PLANE * PASS, HD), bias)
            return carry

        lax.fori_loop(0, KVH, one, 0)

    def use_anchor():
        def one(g, carry):
            update(g, anchor[g], anchor[KVH + g], None)
            return carry

        lax.fori_loop(0, KVH, one, 0)

    lax.fori_loop(0, KVH, own, 0)

    last = plane + 1

    def step(t, carry):
        def at_stage(s, packets, block):
            @pl.when((s >= 0) & (s <= plane))
            def _():
                packets(plane - s)

            @pl.when(s == last)
            def _():
                block()

        def issue_packets(q):
            packet(q).arrived(r)
            packet(q).issue()

        def issue_block():
            @pl.when(me > 0)
            def _():
                block0.arrived(r)

            send_line(anchor.at[r], anchor_z_send, anchor_recv.at[r])
            block0.issue()

        def issue_block_later():
            block0.arrived(r)
            block0.issue()

        def issue_any():
            @pl.when(plane == 0)
            def _():
                issue_block()

            @pl.when(plane > 0)
            def _():
                issue_block_later()

        def compute_packets(q):
            packet(q).gathered()
            use_packets(q)

        def compute_block():
            block0.gathered()

            @pl.when(me > 0)
            def _():
                use_anchor()

        at_stage(t, issue_packets, issue_any)
        at_stage(t - 1, lambda q: packet(q).relay(), block0.relay)
        at_stage(t - 2, lambda q: packet(q).finish(), block0.finish)
        at_stage(t - 3, compute_packets, compute_block)
        return carry

    lax.fori_loop(1, last + 4, step, 0)

    for g in range(KVH):
        out = acc[g] / jnp.sum(tot[g], axis=1, keepdims=True)
        for j in range(GROUP):
            h = g * GROUP + j
            o_ref[:, h * HD:(h + 1) * HD] = out[j * TOK_DEV:(j + 1) * TOK_DEV].astype(o_ref.dtype)

    def drain(q, carry):
        packet(q).sent()
        return carry

    lax.fori_loop(0, plane + 1, drain, 0)
    block0.sent()
    sent_line(buf.at[me], z_send, packet_recv.at[me])

    @pl.when(plane == 0)
    def _():
        sent_line(anchor.at[r], anchor_z_send, anchor_recv.at[r])

    @pl.when(me == 0)
    def _():
        for j in range(1, PLANE):
            scatter(j).wait_send()


def body(n, queries, keys, values, selected):
    planes = n // PLANE
    rows = GROUP * TOK_DEV
    vmem = pl.BlockSpec(memory_space=pltpu.VMEM)
    return pl.pallas_call(
        functools.partial(kernel, n),
        out_shape=jax.ShapeDtypeStruct((TOK_DEV, QH * HD), jnp.bfloat16),
        in_specs=[vmem] * 4,
        out_specs=vmem,
        scratch_shapes=[
            pltpu.VMEM((n, 2 * KVH, PASS, HD), jnp.bfloat16),
            pltpu.VMEM((PLANE, TOK_DEV, HD), jnp.bfloat16),
            pltpu.VMEM((KVH, rows, HD), jnp.float32),
            pltpu.VMEM((KVH, rows, HD), jnp.float32),
            pltpu.VMEM((KVH, rows, HD), jnp.float32),
            pltpu.SemaphoreType.DMA((n,)),
            pltpu.SemaphoreType.DMA((PLANE,)),
            pltpu.SemaphoreType.DMA((planes, 7)),
            pltpu.SemaphoreType.DMA((7,)),
            pltpu.SemaphoreType.DMA((planes,)),
            pltpu.SemaphoreType.DMA((planes,)),
            pltpu.SemaphoreType.DMA((PLANE,)),
        ],
        compiler_params=pltpu.CompilerParams(
            collective_id=0, has_side_effects=True, vmem_limit_bytes=48 * 1024 * 1024),
        cost_estimate=pl.CostEstimate(flops=1300000000, bytes_accessed=4000000, transcendentals=2500000),
    )(queries, keys, values, selected)


def solution(mesh):
    placed = (P("seq", None), P("seq", None), P("seq", None), P("seq", None, None))
    return jax.shard_map(
        functools.partial(body, mesh.shape["seq"]), mesh=mesh, in_specs=placed,
        out_specs=P("seq", None), check_vma=False)
```

```python
import functools
import math

import jax
import jax.numpy as jnp
from jax import lax
from jax.experimental import pallas as pl
from jax.experimental.pallas import tpu as pltpu
from jax.sharding import PartitionSpec as P

HD = 128
QH = 16
KVH = 4
PASS = 32
TOK_DEV = 128
GROUP = QH // KVH
PLANE = 8
LOG2_SCALE = math.log2(math.e) / math.sqrt(HD)
very_negative = -1e30
MESH = pl.DeviceIdType.MESH


def dot_t(a, b):
    return lax.dot_general(a, b, (((1,), (1,)), ((), ())), preferred_element_type=jnp.float32)


def dot(a, b):
    return lax.dot_general(a, b, (((1,), (0,)), ((), ())), preferred_element_type=jnp.float32)


def kernel(n, q_hbm, k_hbm, v_hbm, sel_hbm, o_ref, q_ref, k_ref, v_ref, sel_ref, buf, anchor, acc, best, tot,
           packet_recv, anchor_recv, packet_send, anchor_send, scatter_send, load_sem):
    planes = n // PLANE
    me = lax.axis_index("seq")
    plane = me // PLANE
    r = me % PLANE
    core = r % 2
    x = (r // 2) % 2
    y = r // 4
    near_x = r + 2 - 4 * x
    near_y = r + 4 - 8 * y
    first = near_x * (1 - core) + near_y * core
    second = near_y * (1 - core) + near_x * core
    across = near_x + near_y - r
    to_sib = 1 - 2 * core
    home = plane * PLANE

    barrier = pltpu.get_barrier_semaphore()

    loads = [pltpu.make_async_copy(src, dst, load_sem.at[i]) for i, (src, dst) in enumerate(
        ((sel_hbm, sel_ref), (k_hbm, k_ref), (v_hbm, v_ref), (q_hbm, q_ref)))]
    for load in loads:
        load.start()

    def greet(device):
        pl.semaphore_signal(barrier, inc=1, device_id=(device,), device_id_type=MESH)

    for near in (near_x, near_y, r + to_sib):
        greet(home + near)

    @pl.when(plane > 0)
    def _():
        greet(me - PLANE)

    @pl.when(plane < planes - 1)
    def _():
        greet(me + PLANE)

    is_far = (plane == 0) & (core + x + y >= 2)

    @pl.when(me == 0)
    def _():
        for far in (3, 5, 6, 7):
            greet(far)

    @pl.when(is_far)
    def _():
        greet(0)

    for load in loads[:3]:
        load.wait()

    lane = lax.broadcasted_iota(jnp.int32, (PASS, PASS), 1)
    row = lax.broadcasted_iota(jnp.int32, (PASS, PASS), 0)
    token = lax.broadcasted_iota(jnp.int32, (PASS, TOK_DEV), 1).astype(jnp.float32)
    for g in range(KVH):
        sel = sel_ref[0, g:g + 1, :].astype(jnp.float32)
        column = jnp.sum(jnp.where(lane == row, sel, 0.0), axis=1, keepdims=True)
        one_hot = jnp.where(token == column, 1.0, 0.0).astype(jnp.bfloat16)
        cols = slice(g * HD, (g + 1) * HD)
        buf[me, g] = dot(one_hot, k_ref[:, cols]).astype(jnp.bfloat16)
        buf[me, KVH + g] = dot(one_hot, v_ref[:, cols]).astype(jnp.bfloat16)

    peers = (3 + jnp.where(plane > 0, 1, 0) + jnp.where(plane < planes - 1, 1, 0)
             + jnp.where(me == 0, 4, 0) + jnp.where(is_far, 1, 0))
    pl.semaphore_wait(barrier, peers)

    def remote(ref, send_sem, recv_sem, device):
        return pltpu.make_async_remote_copy(
            src_ref=ref, dst_ref=ref, send_sem=send_sem, recv_sem=recv_sem,
            device_id=(device,), device_id_type=MESH)

    class Stage:
        def __init__(self, piece, recv, send):
            self.piece, self.recv, self.send = piece, recv, send

        def arrived(self, rr):
            remote(self.piece(rr), self.send(0), self.recv(rr), home + first).wait_recv()

        def push(self, rr, target, i):
            remote(self.piece(rr), self.send(i), self.recv(rr), home + target).start()

        def issue(self):
            @pl.when(plane < planes - 1)
            def _():
                remote(self.piece(r), self.send(7), self.recv(r), me + PLANE).start()

            self.push(r, first, 0)
            self.push(r, second, 1)
            self.push(r, r + to_sib, 2)

        def relay(self):
            self.arrived(first)
            self.push(first, second, 3)
            self.push(first, r + to_sib, 4)
            self.arrived(second)
            self.push(second, r + to_sib, 5)

        def finish(self):
            self.arrived(across)
            self.push(across, r + to_sib, 6)

        def gathered(self):
            for rr in (r, first, second, across):
                self.arrived(rr + to_sib)

        def sent(self):
            for i in range(7):
                remote(self.piece(r), self.send(i), self.recv(r), home + first).wait_send()

            @pl.when(plane < planes - 1)
            def _():
                remote(self.piece(r), self.send(7), self.recv(r), me + PLANE).wait_send()

    def packet(q):
        return Stage(lambda rr: buf.at[q * PLANE + rr], lambda rr: packet_recv.at[q * PLANE + rr],
                     lambda i: packet_send.at[q, i])

    block0 = Stage(lambda rr: anchor.at[rr], lambda rr: anchor_recv.at[rr], lambda i: anchor_send.at[i])

    def scatter(j):
        source = k_ref if j < KVH else v_ref
        cols = pl.ds((j % KVH) * HD, HD)
        return pltpu.make_async_remote_copy(
            src_ref=source.at[:, cols], dst_ref=anchor.at[j], send_sem=scatter_send.at[j],
            recv_sem=anchor_recv.at[j], device_id=(j,), device_id_type=MESH)

    @pl.when(me == 0)
    def _():
        for j in range(1, PLANE):
            scatter(j).start()
        anchor[0] = k_ref[:, :HD]

    packet(plane).issue()

    def head_queries(g):
        return jnp.concatenate(
            [q_ref[:, pl.ds(pl.multiple_of((g * GROUP + j) * HD, HD), HD)] for j in range(GROUP)], axis=0)

    def lane_tiles(w):
        return [w[:, i * HD:(i + 1) * HD] for i in range(w.shape[1] // HD)]

    rows = GROUP * TOK_DEV

    def own(g, carry):
        cols = pl.ds(pl.multiple_of(g * HD, HD), HD)
        s = dot_t(head_queries(g), k_ref[:, cols]) * LOG2_SCALE
        position = lax.broadcasted_iota(jnp.int32, (rows, TOK_DEV), 0) % TOK_DEV
        key_at = lax.broadcasted_iota(jnp.int32, (rows, TOK_DEV), 1)
        s = jnp.where(key_at <= position, s, very_negative)
        top = jnp.broadcast_to(jnp.max(s, axis=1, keepdims=True), (rows, HD))
        w = jnp.exp2(s - top)
        best[g] = top
        tot[g] = w
        acc[g] = dot(w.astype(jnp.bfloat16), v_ref[:, cols])
        return carry

    def update(g, key_rows, value_rows, bias):
        s = dot_t(head_queries(g), key_rows) * LOG2_SCALE
        if bias is not None:
            s = s + bias
        tiles = lane_tiles(s)
        old = best[g]
        top = jnp.max(functools.reduce(jnp.maximum, tiles), axis=1, keepdims=True)
        top = jnp.maximum(old, top)
        w = [jnp.exp2(t - top) for t in tiles]
        rescale = jnp.exp2(old - top)
        best[g] = top
        tot[g] = tot[g] * rescale + functools.reduce(jnp.add, w)
        w = jnp.concatenate([t.astype(jnp.bfloat16) for t in w], axis=1)
        acc[g] = acc[g] * rescale + dot(w, value_rows)

    def use_packets(q):
        source = q * PLANE + lax.broadcasted_iota(jnp.int32, (1, PLANE * PASS), 1) // PASS
        bias = jnp.where((source >= 1) & (source < me), 0.0, very_negative)
        at = pl.ds(q * PLANE, PLANE)

        def one(g, carry):
            update(g, buf[at, g].reshape(PLANE * PASS, HD), buf[at, KVH + g].reshape(PLANE * PASS, HD), bias)
            return carry

        lax.fori_loop(0, KVH, one, 0)

    def use_anchor():
        def one(g, carry):
            update(g, anchor[g], anchor[KVH + g], None)
            return carry

        lax.fori_loop(0, KVH, one, 0)

    loads[3].wait()
    lax.fori_loop(0, KVH, own, 0)

    last = plane + 1

    def step(t, carry):
        def at_stage(s, packets, block):
            @pl.when((s >= 0) & (s <= plane))
            def _():
                packets(plane - s)

            @pl.when(s == last)
            def _():
                block()

        def issue_packets(q):
            packet(q).arrived(r)
            packet(q).issue()

        def issue_block():
            @pl.when(me > 0)
            def _():
                block0.arrived(r)

            block0.issue()

        def compute_packets(q):
            packet(q).gathered()
            use_packets(q)

        def compute_block():
            block0.gathered()

            @pl.when(me > 0)
            def _():
                use_anchor()

        at_stage(t, issue_packets, issue_block)
        at_stage(t - 1, lambda q: packet(q).relay(), block0.relay)
        at_stage(t - 2, lambda q: packet(q).finish(), block0.finish)
        at_stage(t - 3, compute_packets, compute_block)
        return carry

    lax.fori_loop(1, last + 4, step, 0)

    for g in range(KVH):
        out = acc[g] / jnp.sum(tot[g], axis=1, keepdims=True)
        for j in range(GROUP):
            h = g * GROUP + j
            o_ref[:, h * HD:(h + 1) * HD] = out[j * TOK_DEV:(j + 1) * TOK_DEV].astype(o_ref.dtype)

    def drain(q, carry):
        packet(q).sent()
        return carry

    lax.fori_loop(0, plane + 1, drain, 0)
    block0.sent()

    @pl.when(me == 0)
    def _():
        for j in range(1, PLANE):
            scatter(j).wait_send()


def body(n, queries, keys, values, selected):
    planes = n // PLANE
    rows = GROUP * TOK_DEV
    vmem = pl.BlockSpec(memory_space=pltpu.VMEM)
    return pl.pallas_call(
        functools.partial(kernel, n),
        out_shape=jax.ShapeDtypeStruct((TOK_DEV, QH * HD), jnp.bfloat16),
        in_specs=[pl.BlockSpec(memory_space=pltpu.HBM)] * 4,
        out_specs=vmem,
        scratch_shapes=[
            pltpu.VMEM(queries.shape, queries.dtype),
            pltpu.VMEM(keys.shape, keys.dtype),
            pltpu.VMEM(values.shape, values.dtype),
            pltpu.VMEM(selected.shape, selected.dtype),
            pltpu.VMEM((n, 2 * KVH, PASS, HD), jnp.bfloat16),
            pltpu.VMEM((PLANE, TOK_DEV, HD), jnp.bfloat16),
            pltpu.VMEM((KVH, rows, HD), jnp.float32),
            pltpu.VMEM((KVH, rows, HD), jnp.float32),
            pltpu.VMEM((KVH, rows, HD), jnp.float32),
            pltpu.SemaphoreType.DMA((n,)),
            pltpu.SemaphoreType.DMA((PLANE,)),
            pltpu.SemaphoreType.DMA((planes, 8)),
            pltpu.SemaphoreType.DMA((8,)),
            pltpu.SemaphoreType.DMA((PLANE,)),
            pltpu.SemaphoreType.DMA((4,)),
        ],
        compiler_params=pltpu.CompilerParams(
            collective_id=0, has_side_effects=True, vmem_limit_bytes=48 * 1024 * 1024),
        cost_estimate=pl.CostEstimate(flops=1300000000, bytes_accessed=4000000, transcendentals=2500000),
    )(queries, keys, values, selected)


def solution(mesh):
    placed = (P("seq", None), P("seq", None), P("seq", None), P("seq", None, None))
    return jax.shard_map(
        functools.partial(body, mesh.shape["seq"]), mesh=mesh, in_specs=placed,
        out_specs=P("seq", None), check_vma=False)
```

```python
import functools
import math

import jax
import jax.numpy as jnp
from jax import lax
from jax.experimental import pallas as pl
from jax.experimental.pallas import tpu as pltpu
from jax.sharding import PartitionSpec as P

HD = 128
QH = 16
KVH = 4
PASS = 32
TOK_DEV = 128
GROUP = QH // KVH
PLANE = 8
LOG2_SCALE = math.log2(math.e) / math.sqrt(HD)
very_negative = -1e30
MESH = pl.DeviceIdType.MESH


def dot_t(a, b):
    return lax.dot_general(a, b, (((1,), (1,)), ((), ())), preferred_element_type=jnp.float32)


def dot(a, b):
    return lax.dot_general(a, b, (((1,), (0,)), ((), ())), preferred_element_type=jnp.float32)


def kernel(n, q_hbm, k_hbm, v_hbm, sel_hbm, o_ref, q_ref, k_ref, v_ref, sel_ref, buf, anchor, acc, best, tot,
           packet_recv, anchor_recv, packet_send, anchor_send, scatter_send, load_sem):
    planes = n // PLANE
    me = lax.axis_index("seq")
    plane = me // PLANE
    r = me % PLANE
    core = r % 2
    x = (r // 2) % 2
    y = r // 4
    near_x = r + 2 - 4 * x
    near_y = r + 4 - 8 * y
    first = near_x * (1 - core) + near_y * core
    second = near_y * (1 - core) + near_x * core
    across = near_x + near_y - r
    to_sib = 1 - 2 * core
    home = plane * PLANE

    barrier = pltpu.get_barrier_semaphore()

    loads = [pltpu.make_async_copy(src, dst, load_sem.at[i]) for i, (src, dst) in enumerate(
        ((sel_hbm, sel_ref), (k_hbm, k_ref), (v_hbm, v_ref), (q_hbm, q_ref)))]
    for load in loads:
        load.start()

    def greet(device):
        pl.semaphore_signal(barrier, inc=1, device_id=(device,), device_id_type=MESH)

    for near in (near_x, near_y, r + to_sib):
        greet(home + near)

    @pl.when(plane > 0)
    def _():
        greet(me - PLANE)

    @pl.when(plane < planes - 1)
    def _():
        greet(me + PLANE)

    is_far = (plane == 0) & (core + x + y >= 2)

    @pl.when(me == 0)
    def _():
        for far in (3, 5, 6, 7):
            greet(far)

    @pl.when(is_far)
    def _():
        greet(0)

    for load in loads[:3]:
        load.wait()

    lane = lax.broadcasted_iota(jnp.int32, (PASS, PASS), 1)
    row = lax.broadcasted_iota(jnp.int32, (PASS, PASS), 0)
    token = lax.broadcasted_iota(jnp.int32, (PASS, TOK_DEV), 1).astype(jnp.float32)
    for g in range(KVH):
        sel = sel_ref[0, g:g + 1, :].astype(jnp.float32)
        column = jnp.sum(jnp.where(lane == row, sel, 0.0), axis=1, keepdims=True)
        one_hot = jnp.where(token == column, 1.0, 0.0).astype(jnp.bfloat16)
        cols = slice(g * HD, (g + 1) * HD)
        buf[me, g] = dot(one_hot, k_ref[:, cols]).astype(jnp.bfloat16)
        buf[me, KVH + g] = dot(one_hot, v_ref[:, cols]).astype(jnp.bfloat16)

    peers = (3 + jnp.where(plane > 0, 1, 0) + jnp.where(plane < planes - 1, 1, 0)
             + jnp.where(me == 0, 4, 0) + jnp.where(is_far, 1, 0))
    pl.semaphore_wait(barrier, peers)

    def remote(ref, send_sem, recv_sem, device):
        return pltpu.make_async_remote_copy(
            src_ref=ref, dst_ref=ref, send_sem=send_sem, recv_sem=recv_sem,
            device_id=(device,), device_id_type=MESH)

    class Stage:
        def __init__(self, piece, recv, send):
            self.piece, self.recv, self.send = piece, recv, send

        def arrived(self, rr):
            remote(self.piece(rr), self.send(0), self.recv(rr), home + first).wait_recv()

        def push(self, rr, target, i):
            remote(self.piece(rr), self.send(i), self.recv(rr), home + target).start()

        def issue(self):
            @pl.when(plane < planes - 1)
            def _():
                remote(self.piece(r), self.send(7), self.recv(r), me + PLANE).start()

            self.push(r, first, 0)
            self.push(r, second, 1)
            self.push(r, r + to_sib, 2)

        def relay(self):
            self.arrived(first)
            self.push(first, second, 3)
            self.push(first, r + to_sib, 4)
            self.arrived(second)
            self.push(second, r + to_sib, 5)

        def finish(self):
            self.arrived(across)
            self.push(across, r + to_sib, 6)

        def gathered(self):
            for rr in (r, first, second, across):
                self.arrived(rr + to_sib)

        def sent(self):
            for i in range(7):
                remote(self.piece(r), self.send(i), self.recv(r), home + first).wait_send()

            @pl.when(plane < planes - 1)
            def _():
                remote(self.piece(r), self.send(7), self.recv(r), me + PLANE).wait_send()

    def packet(q):
        return Stage(lambda rr: buf.at[q * PLANE + rr], lambda rr: packet_recv.at[q * PLANE + rr],
                     lambda i: packet_send.at[q, i])

    block0 = Stage(lambda rr: anchor.at[rr], lambda rr: anchor_recv.at[rr], lambda i: anchor_send.at[i])

    def scatter(j):
        source = k_ref if j < KVH else v_ref
        cols = pl.ds((j % KVH) * HD, HD)
        return pltpu.make_async_remote_copy(
            src_ref=source.at[:, cols], dst_ref=anchor.at[j], send_sem=scatter_send.at[j],
            recv_sem=anchor_recv.at[j], device_id=(j,), device_id_type=MESH)

    @pl.when(me == 0)
    def _():
        for j in range(1, PLANE):
            scatter(j).start()
        anchor[0] = k_ref[:, :HD]

    packet(plane).issue()

    def head_queries(g):
        return jnp.concatenate(
            [q_ref[:, pl.ds(pl.multiple_of((g * GROUP + j) * HD, HD), HD)] for j in range(GROUP)], axis=0)

    def lane_tiles(w):
        return [w[:, i * HD:(i + 1) * HD] for i in range(w.shape[1] // HD)]

    rows = GROUP * TOK_DEV

    def own(g, carry):
        cols = pl.ds(pl.multiple_of(g * HD, HD), HD)
        s = dot_t(head_queries(g), k_ref[:, cols]) * LOG2_SCALE
        position = lax.broadcasted_iota(jnp.int32, (rows, TOK_DEV), 0) % TOK_DEV
        key_at = lax.broadcasted_iota(jnp.int32, (rows, TOK_DEV), 1)
        s = jnp.where(key_at <= position, s, very_negative)
        top = jnp.broadcast_to(jnp.max(s, axis=1, keepdims=True), (rows, HD))
        w = jnp.exp2(s - top)
        best[g] = top
        tot[g] = w
        acc[g] = dot(w.astype(jnp.bfloat16), v_ref[:, cols])
        return carry

    def update(g, key_rows, value_rows, bias):
        s = dot_t(head_queries(g), key_rows) * LOG2_SCALE
        if bias is not None:
            s = s + bias
        tiles = lane_tiles(s)
        old = best[g]
        top = jnp.max(functools.reduce(jnp.maximum, tiles), axis=1, keepdims=True)
        top = jnp.maximum(old, top)
        w = [jnp.exp2(t - top) for t in tiles]
        rescale = jnp.exp2(old - top)
        best[g] = top
        tot[g] = tot[g] * rescale + functools.reduce(jnp.add, w)
        w = jnp.concatenate([t.astype(jnp.bfloat16) for t in w], axis=1)
        acc[g] = acc[g] * rescale + dot(w, value_rows)

    def use_packets(q):
        source = q * PLANE + lax.broadcasted_iota(jnp.int32, (1, PLANE * PASS), 1) // PASS
        bias = jnp.where((source >= 1) & (source < me), 0.0, very_negative)
        at = pl.ds(q * PLANE, PLANE)

        def one(g, carry):
            update(g, buf[at, g].reshape(PLANE * PASS, HD), buf[at, KVH + g].reshape(PLANE * PASS, HD), bias)
            return carry

        lax.fori_loop(0, KVH, one, 0, unroll=True)

    def use_anchor():
        def one(g, carry):
            update(g, anchor[g], anchor[KVH + g], None)
            return carry

        lax.fori_loop(0, KVH, one, 0, unroll=True)

    loads[3].wait()
    lax.fori_loop(0, KVH, own, 0, unroll=True)

    last = plane + 1

    def step(t, carry):
        def at_stage(s, packets, block):
            @pl.when((s >= 0) & (s <= plane))
            def _():
                packets(plane - s)

            @pl.when(s == last)
            def _():
                block()

        def issue_packets(q):
            packet(q).arrived(r)
            packet(q).issue()

        def issue_block():
            @pl.when(me > 0)
            def _():
                block0.arrived(r)

            block0.issue()

        def compute_packets(q):
            packet(q).gathered()
            use_packets(q)

        def compute_block():
            block0.gathered()

            @pl.when(me > 0)
            def _():
                use_anchor()

        at_stage(t, issue_packets, issue_block)
        at_stage(t - 1, lambda q: packet(q).relay(), block0.relay)
        at_stage(t - 2, lambda q: packet(q).finish(), block0.finish)
        at_stage(t - 3, compute_packets, compute_block)
        return carry

    lax.fori_loop(1, last + 4, step, 0)

    for g in range(KVH):
        out = acc[g] / jnp.sum(tot[g], axis=1, keepdims=True)
        for j in range(GROUP):
            h = g * GROUP + j
            o_ref[:, h * HD:(h + 1) * HD] = out[j * TOK_DEV:(j + 1) * TOK_DEV].astype(o_ref.dtype)

    def drain(q, carry):
        packet(q).sent()
        return carry

    lax.fori_loop(0, plane + 1, drain, 0)
    block0.sent()

    @pl.when(me == 0)
    def _():
        for j in range(1, PLANE):
            scatter(j).wait_send()


def body(n, queries, keys, values, selected):
    planes = n // PLANE
    rows = GROUP * TOK_DEV
    vmem = pl.BlockSpec(memory_space=pltpu.VMEM)
    return pl.pallas_call(
        functools.partial(kernel, n),
        out_shape=jax.ShapeDtypeStruct((TOK_DEV, QH * HD), jnp.bfloat16),
        in_specs=[pl.BlockSpec(memory_space=pltpu.HBM)] * 4,
        out_specs=vmem,
        scratch_shapes=[
            pltpu.VMEM(queries.shape, queries.dtype),
            pltpu.VMEM(keys.shape, keys.dtype),
            pltpu.VMEM(values.shape, values.dtype),
            pltpu.VMEM(selected.shape, selected.dtype),
            pltpu.VMEM((n, 2 * KVH, PASS, HD), jnp.bfloat16),
            pltpu.VMEM((PLANE, TOK_DEV, HD), jnp.bfloat16),
            pltpu.VMEM((KVH, rows, HD), jnp.float32),
            pltpu.VMEM((KVH, rows, HD), jnp.float32),
            pltpu.VMEM((KVH, rows, HD), jnp.float32),
            pltpu.SemaphoreType.DMA((n,)),
            pltpu.SemaphoreType.DMA((PLANE,)),
            pltpu.SemaphoreType.DMA((planes, 8)),
            pltpu.SemaphoreType.DMA((8,)),
            pltpu.SemaphoreType.DMA((PLANE,)),
            pltpu.SemaphoreType.DMA((4,)),
        ],
        compiler_params=pltpu.CompilerParams(
            collective_id=0, has_side_effects=True, vmem_limit_bytes=60 * 1024 * 1024),
        cost_estimate=pl.CostEstimate(flops=1300000000, bytes_accessed=4000000, transcendentals=2500000),
    )(queries, keys, values, selected)


def solution(mesh):
    placed = (P("seq", None), P("seq", None), P("seq", None), P("seq", None, None))
    return jax.shard_map(
        functools.partial(body, mesh.shape["seq"]), mesh=mesh, in_specs=placed,
        out_specs=P("seq", None), check_vma=False)
```

```python
import functools
import math

import jax
import jax.numpy as jnp
from jax import lax
from jax.experimental import pallas as pl
from jax.experimental.pallas import tpu as pltpu
from jax.sharding import PartitionSpec as P

HD = 128
QH = 16
KVH = 4
PASS = 32
TOK_DEV = 128
GROUP = QH // KVH
PLANE = 8
LOG2_SCALE = math.log2(math.e) / math.sqrt(HD)
very_negative = -1e30
MESH = pl.DeviceIdType.MESH


def dot_t(a, b):
    return lax.dot_general(a, b, (((1,), (1,)), ((), ())), preferred_element_type=jnp.float32)


def dot(a, b):
    return lax.dot_general(a, b, (((1,), (0,)), ((), ())), preferred_element_type=jnp.float32)


def kernel(n, q_hbm, k_hbm, v_hbm, sel_hbm, o_ref, q_ref, k_ref, v_ref, sel_ref, buf, anchor, acc, best, tot,
           packet_recv, anchor_recv, packet_send, anchor_send, scatter_send, load_sem):
    planes = n // PLANE
    me = lax.axis_index("seq")
    plane = me // PLANE
    r = me % PLANE
    core = r % 2
    x = (r // 2) % 2
    y = r // 4
    near_x = r + 2 - 4 * x
    near_y = r + 4 - 8 * y
    first = near_x * (1 - core) + near_y * core
    second = near_y * (1 - core) + near_x * core
    across = near_x + near_y - r
    to_sib = 1 - 2 * core
    home = plane * PLANE

    barrier = pltpu.get_barrier_semaphore()

    loads = [pltpu.make_async_copy(src, dst, load_sem.at[i]) for i, (src, dst) in enumerate(
        ((sel_hbm, sel_ref), (k_hbm, k_ref), (v_hbm, v_ref), (q_hbm, q_ref)))]
    for load in loads:
        load.start()

    def greet(device):
        pl.semaphore_signal(barrier, inc=1, device_id=(device,), device_id_type=MESH)

    for near in (near_x, near_y, r + to_sib):
        greet(home + near)

    @pl.when(plane > 0)
    def _():
        greet(me - PLANE)

    @pl.when(plane < planes - 1)
    def _():
        greet(me + PLANE)

    is_far = (plane == 0) & (core + x + y >= 2)

    @pl.when(me == 0)
    def _():
        for far in (3, 5, 6, 7):
            greet(far)

    @pl.when(is_far)
    def _():
        greet(0)

    for load in loads[:3]:
        load.wait()

    lane = lax.broadcasted_iota(jnp.int32, (PASS, PASS), 1)
    row = lax.broadcasted_iota(jnp.int32, (PASS, PASS), 0)
    token = lax.broadcasted_iota(jnp.int32, (PASS, TOK_DEV), 1).astype(jnp.float32)
    for g in range(KVH):
        sel = sel_ref[0, g:g + 1, :].astype(jnp.float32)
        column = jnp.sum(jnp.where(lane == row, sel, 0.0), axis=1, keepdims=True)
        one_hot = jnp.where(token == column, 1.0, 0.0).astype(jnp.bfloat16)
        cols = slice(g * HD, (g + 1) * HD)
        buf[me, g] = dot(one_hot, k_ref[:, cols]).astype(jnp.bfloat16)
        buf[me, KVH + g] = dot(one_hot, v_ref[:, cols]).astype(jnp.bfloat16)

    peers = (3 + jnp.where(plane > 0, 1, 0) + jnp.where(plane < planes - 1, 1, 0)
             + jnp.where(me == 0, 4, 0) + jnp.where(is_far, 1, 0))
    pl.semaphore_wait(barrier, peers)

    def remote(ref, send_sem, recv_sem, device):
        return pltpu.make_async_remote_copy(
            src_ref=ref, dst_ref=ref, send_sem=send_sem, recv_sem=recv_sem,
            device_id=(device,), device_id_type=MESH)

    class Stage:
        def __init__(self, piece, recv, send):
            self.piece, self.recv, self.send = piece, recv, send

        def arrived(self, rr):
            remote(self.piece(rr), self.send(0), self.recv(rr), home + first).wait_recv()

        def push(self, rr, target, i):
            remote(self.piece(rr), self.send(i), self.recv(rr), home + target).start()

        def issue(self):
            @pl.when(plane < planes - 1)
            def _():
                remote(self.piece(r), self.send(7), self.recv(r), me + PLANE).start()

            self.push(r, first, 0)
            self.push(r, second, 1)
            self.push(r, r + to_sib, 2)

        def relay(self):
            self.arrived(first)
            self.push(first, second, 3)
            self.push(first, r + to_sib, 4)
            self.arrived(second)
            self.push(second, r + to_sib, 5)

        def finish(self):
            self.arrived(across)
            self.push(across, r + to_sib, 6)

        def gathered(self):
            for rr in (r, first, second, across):
                self.arrived(rr + to_sib)

        def sent(self):
            for i in range(7):
                remote(self.piece(r), self.send(i), self.recv(r), home + first).wait_send()

            @pl.when(plane < planes - 1)
            def _():
                remote(self.piece(r), self.send(7), self.recv(r), me + PLANE).wait_send()

    def packet(q):
        return Stage(lambda rr: buf.at[q * PLANE + rr], lambda rr: packet_recv.at[q * PLANE + rr],
                     lambda i: packet_send.at[q, i])

    block0 = Stage(lambda rr: anchor.at[rr], lambda rr: anchor_recv.at[rr], lambda i: anchor_send.at[i])

    def scatter(j):
        source = k_ref if j < KVH else v_ref
        cols = pl.ds((j % KVH) * HD, HD)
        return pltpu.make_async_remote_copy(
            src_ref=source.at[:, cols], dst_ref=anchor.at[j], send_sem=scatter_send.at[j],
            recv_sem=anchor_recv.at[j], device_id=(j,), device_id_type=MESH)

    @pl.when(me == 0)
    def _():
        for j in range(1, PLANE):
            scatter(j).start()
        anchor[0] = k_ref[:, :HD]

    packet(plane).issue()

    def head_queries(g):
        return jnp.concatenate(
            [q_ref[:, pl.ds(pl.multiple_of((g * GROUP + j) * HD, HD), HD)] for j in range(GROUP)], axis=0)

    def lane_tiles(w):
        return [w[:, i * HD:(i + 1) * HD] for i in range(w.shape[1] // HD)]

    rows = GROUP * TOK_DEV

    def own(g, carry):
        cols = pl.ds(pl.multiple_of(g * HD, HD), HD)
        s = dot_t(head_queries(g), k_ref[:, cols]) * LOG2_SCALE
        position = lax.broadcasted_iota(jnp.int32, (rows, TOK_DEV), 0) % TOK_DEV
        key_at = lax.broadcasted_iota(jnp.int32, (rows, TOK_DEV), 1)
        s = jnp.where(key_at <= position, s, very_negative)
        top = jnp.broadcast_to(jnp.max(s, axis=1, keepdims=True), (rows, HD))
        w = jnp.exp2(s - top)
        best[g] = top
        tot[g] = w
        acc[g] = dot(w.astype(jnp.bfloat16), v_ref[:, cols])
        return carry

    def update(g, key_rows, value_rows, bias):
        s = dot_t(head_queries(g), key_rows) * LOG2_SCALE
        if bias is not None:
            s = s + bias
        tiles = lane_tiles(s)
        old = best[g]
        top = jnp.max(functools.reduce(jnp.maximum, tiles), axis=1, keepdims=True)
        top = jnp.maximum(old, top)
        w = [jnp.exp2(t - top) for t in tiles]
        rescale = jnp.exp2(old - top)
        best[g] = top
        tot[g] = tot[g] * rescale + functools.reduce(jnp.add, w)
        w = jnp.concatenate([t.astype(jnp.bfloat16) for t in w], axis=1)
        acc[g] = acc[g] * rescale + dot(w, value_rows)

    def use_packets(q):
        source = q * PLANE + lax.broadcasted_iota(jnp.int32, (1, PLANE * PASS), 1) // PASS
        bias = jnp.where((source >= 1) & (source < me), 0.0, very_negative)
        at = pl.ds(q * PLANE, PLANE)

        def one(g, carry):
            update(g, buf[at, g].reshape(PLANE * PASS, HD), buf[at, KVH + g].reshape(PLANE * PASS, HD), bias)
            return carry

        lax.fori_loop(0, KVH, one, 0, unroll=True)

    def use_anchor():
        def one(g, carry):
            update(g, anchor[g], anchor[KVH + g], None)
            return carry

        lax.fori_loop(0, KVH, one, 0, unroll=True)

    loads[3].wait()
    lax.fori_loop(0, KVH, own, 0, unroll=True)

    last = plane + 1

    def step(t, carry):
        def at_stage(s, packets, block):
            @pl.when((s >= 0) & (s <= plane))
            def _():
                packets(plane - s)

            @pl.when(s == last)
            def _():
                block()

        def issue_packets(q):
            packet(q).arrived(r)
            packet(q).issue()

        def issue_block():
            @pl.when(me > 0)
            def _():
                block0.arrived(r)

            block0.issue()

        def compute_packets(q):
            packet(q).gathered()
            use_packets(q)

        def compute_block():
            block0.gathered()

            @pl.when(me > 0)
            def _():
                use_anchor()

        at_stage(t, issue_packets, issue_block)
        at_stage(t - 1, lambda q: packet(q).relay(), block0.relay)
        at_stage(t - 3, compute_packets, compute_block)
        at_stage(t - 2, lambda q: packet(q).finish(), block0.finish)
        return carry

    lax.fori_loop(1, last + 4, step, 0)

    for g in range(KVH):
        out = acc[g] / jnp.sum(tot[g], axis=1, keepdims=True)
        for j in range(GROUP):
            h = g * GROUP + j
            o_ref[:, h * HD:(h + 1) * HD] = out[j * TOK_DEV:(j + 1) * TOK_DEV].astype(o_ref.dtype)

    def drain(q, carry):
        packet(q).sent()
        return carry

    lax.fori_loop(0, plane + 1, drain, 0)
    block0.sent()

    @pl.when(me == 0)
    def _():
        for j in range(1, PLANE):
            scatter(j).wait_send()


def body(n, queries, keys, values, selected):
    planes = n // PLANE
    rows = GROUP * TOK_DEV
    vmem = pl.BlockSpec(memory_space=pltpu.VMEM)
    return pl.pallas_call(
        functools.partial(kernel, n),
        out_shape=jax.ShapeDtypeStruct((TOK_DEV, QH * HD), jnp.bfloat16),
        in_specs=[pl.BlockSpec(memory_space=pltpu.HBM)] * 4,
        out_specs=vmem,
        scratch_shapes=[
            pltpu.VMEM(queries.shape, queries.dtype),
            pltpu.VMEM(keys.shape, keys.dtype),
            pltpu.VMEM(values.shape, values.dtype),
            pltpu.VMEM(selected.shape, selected.dtype),
            pltpu.VMEM((n, 2 * KVH, PASS, HD), jnp.bfloat16),
            pltpu.VMEM((PLANE, TOK_DEV, HD), jnp.bfloat16),
            pltpu.VMEM((KVH, rows, HD), jnp.float32),
            pltpu.VMEM((KVH, rows, HD), jnp.float32),
            pltpu.VMEM((KVH, rows, HD), jnp.float32),
            pltpu.SemaphoreType.DMA((n,)),
            pltpu.SemaphoreType.DMA((PLANE,)),
            pltpu.SemaphoreType.DMA((planes, 8)),
            pltpu.SemaphoreType.DMA((8,)),
            pltpu.SemaphoreType.DMA((PLANE,)),
            pltpu.SemaphoreType.DMA((4,)),
        ],
        compiler_params=pltpu.CompilerParams(
            collective_id=0, has_side_effects=True, vmem_limit_bytes=60 * 1024 * 1024),
        cost_estimate=pl.CostEstimate(flops=1300000000, bytes_accessed=4000000, transcendentals=2500000),
    )(queries, keys, values, selected)


def solution(mesh):
    placed = (P("seq", None), P("seq", None), P("seq", None), P("seq", None, None))
    return jax.shard_map(
        functools.partial(body, mesh.shape["seq"]), mesh=mesh, in_specs=placed,
        out_specs=P("seq", None), check_vma=False)
```

```python
import functools
import math

import jax
import jax.numpy as jnp
from jax import lax
from jax.experimental import pallas as pl
from jax.experimental.pallas import tpu as pltpu
from jax.sharding import PartitionSpec as P

HD = 128
QH = 16
KVH = 4
PASS = 32
TOK_DEV = 128
GROUP = QH // KVH
PLANE = 8
LOG2_SCALE = math.log2(math.e) / math.sqrt(HD)
very_negative = -1e30
MESH = pl.DeviceIdType.MESH


def dot_t(a, b):
    return lax.dot_general(a, b, (((1,), (1,)), ((), ())), preferred_element_type=jnp.float32)


def dot(a, b):
    return lax.dot_general(a, b, (((1,), (0,)), ((), ())), preferred_element_type=jnp.float32)


def kernel(n, q_hbm, k_hbm, v_hbm, sel_hbm, o_ref, q_ref, k_ref, v_ref, sel_ref, buf, anchor, acc, best, tot,
           packet_recv, anchor_recv, packet_send, anchor_send, scatter_send, load_sem):
    planes = n // PLANE
    me = lax.axis_index("seq")
    plane = me // PLANE
    r = me % PLANE
    core = r % 2
    x = (r // 2) % 2
    y = r // 4
    near_x = r + 2 - 4 * x
    near_y = r + 4 - 8 * y
    first = near_x * (1 - core) + near_y * core
    second = near_y * (1 - core) + near_x * core
    across = near_x + near_y - r
    to_sib = 1 - 2 * core
    home = plane * PLANE

    barrier = pltpu.get_barrier_semaphore()

    loads = [pltpu.make_async_copy(src, dst, load_sem.at[i]) for i, (src, dst) in enumerate(
        ((sel_hbm, sel_ref), (k_hbm, k_ref), (v_hbm, v_ref), (q_hbm, q_ref)))]
    for load in loads:
        load.start()

    def greet(device):
        pl.semaphore_signal(barrier, inc=1, device_id=(device,), device_id_type=MESH)

    for near in (near_x, near_y, r + to_sib):
        greet(home + near)

    @pl.when(plane > 0)
    def _():
        greet(me - PLANE)

    @pl.when(plane < planes - 1)
    def _():
        greet(me + PLANE)

    is_far = (plane == 0) & (core + x + y >= 2)

    @pl.when(me == 0)
    def _():
        for far in (3, 5, 6, 7):
            greet(far)

    @pl.when(is_far)
    def _():
        greet(0)

    for load in loads[:3]:
        load.wait()

    lane = lax.broadcasted_iota(jnp.int32, (PASS, PASS), 1)
    row = lax.broadcasted_iota(jnp.int32, (PASS, PASS), 0)
    token = lax.broadcasted_iota(jnp.int32, (PASS, TOK_DEV), 1).astype(jnp.float32)
    for g in range(KVH):
        sel = sel_ref[0, g:g + 1, :].astype(jnp.float32)
        column = jnp.sum(jnp.where(lane == row, sel, 0.0), axis=1, keepdims=True)
        one_hot = jnp.where(token == column, 1.0, 0.0).astype(jnp.bfloat16)
        cols = slice(g * HD, (g + 1) * HD)
        buf[me, g] = dot(one_hot, k_ref[:, cols]).astype(jnp.bfloat16)
        buf[me, KVH + g] = dot(one_hot, v_ref[:, cols]).astype(jnp.bfloat16)

    peers = (3 + jnp.where(plane > 0, 1, 0) + jnp.where(plane < planes - 1, 1, 0)
             + jnp.where(me == 0, 4, 0) + jnp.where(is_far, 1, 0))
    pl.semaphore_wait(barrier, peers)

    def remote(ref, send_sem, recv_sem, device):
        return pltpu.make_async_remote_copy(
            src_ref=ref, dst_ref=ref, send_sem=send_sem, recv_sem=recv_sem,
            device_id=(device,), device_id_type=MESH)

    class Stage:
        def __init__(self, piece, recv, send):
            self.piece, self.recv, self.send = piece, recv, send

        def arrived(self, rr):
            remote(self.piece(rr), self.send(0), self.recv(rr), home + first).wait_recv()

        def push(self, rr, target, i):
            remote(self.piece(rr), self.send(i), self.recv(rr), home + target).start()

        def issue(self):
            @pl.when(plane < planes - 1)
            def _():
                remote(self.piece(r), self.send(7), self.recv(r), me + PLANE).start()

            self.push(r, first, 0)
            self.push(r, second, 1)
            self.push(r, r + to_sib, 2)

        def relay(self):
            self.arrived(first)
            self.push(first, second, 3)
            self.push(first, r + to_sib, 4)
            self.arrived(second)
            self.push(second, r + to_sib, 5)

        def finish(self):
            self.arrived(across)
            self.push(across, r + to_sib, 6)

        def gathered(self):
            for rr in (r, first, second, across):
                self.arrived(rr + to_sib)

        def sent(self):
            for i in range(7):
                remote(self.piece(r), self.send(i), self.recv(r), home + first).wait_send()

            @pl.when(plane < planes - 1)
            def _():
                remote(self.piece(r), self.send(7), self.recv(r), me + PLANE).wait_send()

    def packet(q):
        return Stage(lambda rr: buf.at[q * PLANE + rr], lambda rr: packet_recv.at[q * PLANE + rr],
                     lambda i: packet_send.at[q, i])

    block0 = Stage(lambda rr: anchor.at[rr], lambda rr: anchor_recv.at[rr], lambda i: anchor_send.at[i])

    def scatter(j):
        source = k_ref if j < KVH else v_ref
        cols = pl.ds((j % KVH) * HD, HD)
        return pltpu.make_async_remote_copy(
            src_ref=source.at[:, cols], dst_ref=anchor.at[j], send_sem=scatter_send.at[j],
            recv_sem=anchor_recv.at[j], device_id=(j,), device_id_type=MESH)

    @pl.when(me == 0)
    def _():
        for j in range(1, PLANE):
            scatter(j).start()
        anchor[0] = k_ref[:, :HD]

    packet(plane).issue()

    def head_queries(g):
        return jnp.concatenate(
            [q_ref[:, pl.ds(pl.multiple_of((g * GROUP + j) * HD, HD), HD)] for j in range(GROUP)], axis=0)

    def lane_tiles(w):
        return [w[:, i * HD:(i + 1) * HD] for i in range(w.shape[1] // HD)]

    rows = GROUP * TOK_DEV

    def own(g, carry):
        cols = pl.ds(pl.multiple_of(g * HD, HD), HD)
        s = dot_t(head_queries(g), k_ref[:, cols]) * LOG2_SCALE
        position = lax.broadcasted_iota(jnp.int32, (rows, TOK_DEV), 0) % TOK_DEV
        key_at = lax.broadcasted_iota(jnp.int32, (rows, TOK_DEV), 1)
        s = jnp.where(key_at <= position, s, very_negative)
        top = jnp.broadcast_to(jnp.max(s, axis=1, keepdims=True), (rows, HD))
        w = jnp.exp2(s - top)
        best[g] = top
        tot[g] = w
        acc[g] = dot(w.astype(jnp.bfloat16), v_ref[:, cols])
        return carry

    def update(g, key_rows, value_rows, bias):
        s = dot_t(head_queries(g), key_rows) * LOG2_SCALE
        if bias is not None:
            s = s + bias
        tiles = lane_tiles(s)
        old = best[g]
        top = jnp.max(functools.reduce(jnp.maximum, tiles), axis=1, keepdims=True)
        top = jnp.maximum(old, top)
        w = [jnp.exp2(t - top) for t in tiles]
        rescale = jnp.exp2(old - top)
        best[g] = top
        tot[g] = tot[g] * rescale + functools.reduce(jnp.add, w)
        w = jnp.concatenate([t.astype(jnp.bfloat16) for t in w], axis=1)
        acc[g] = acc[g] * rescale + dot(w, value_rows)

    def use_packets(q):
        source = q * PLANE + lax.broadcasted_iota(jnp.int32, (1, PLANE * PASS), 1) // PASS
        bias = jnp.where((source >= 1) & (source < me), 0.0, very_negative)
        at = pl.ds(q * PLANE, PLANE)

        def one(g, carry):
            update(g, buf[at, g].reshape(PLANE * PASS, HD), buf[at, KVH + g].reshape(PLANE * PASS, HD), bias)
            return carry

        lax.fori_loop(0, KVH, one, 0, unroll=True)

    def use_anchor(head):
        for i in range(2):
            update(head + i, anchor[head + i], anchor[KVH + head + i], None)

    loads[3].wait()
    lax.fori_loop(0, KVH, own, 0, unroll=True)

    last = plane + 1

    def step(t, carry):
        def at_stage(s, packets, block):
            @pl.when((s >= 0) & (s <= plane))
            def _():
                packets(plane - s)

            @pl.when(s == last)
            def _():
                block()

        def issue_packets(q):
            packet(q).arrived(r)
            packet(q).issue()

        def issue_block():
            @pl.when(me > 0)
            def _():
                block0.arrived(r)

            block0.issue()

        def compute_packets(q):
            packet(q).gathered()
            use_packets(q)

        def compute_block():
            for rr, other, column in ((r, near_y, x), (near_x, across, 1 - x)):
                block0.arrived(rr + to_sib)
                block0.arrived(other + to_sib)

                @pl.when(me > 0)
                def _():
                    use_anchor(2 * column)

        at_stage(t, issue_packets, issue_block)
        at_stage(t - 1, lambda q: packet(q).relay(), block0.relay)
        at_stage(t - 3, compute_packets, compute_block)
        at_stage(t - 2, lambda q: packet(q).finish(), block0.finish)
        return carry

    lax.fori_loop(1, last + 4, step, 0)

    for g in range(KVH):
        out = acc[g] / jnp.sum(tot[g], axis=1, keepdims=True)
        for j in range(GROUP):
            h = g * GROUP + j
            o_ref[:, h * HD:(h + 1) * HD] = out[j * TOK_DEV:(j + 1) * TOK_DEV].astype(o_ref.dtype)

    def drain(q, carry):
        packet(q).sent()
        return carry

    lax.fori_loop(0, plane + 1, drain, 0)
    block0.sent()

    @pl.when(me == 0)
    def _():
        for j in range(1, PLANE):
            scatter(j).wait_send()


def body(n, queries, keys, values, selected):
    planes = n // PLANE
    rows = GROUP * TOK_DEV
    vmem = pl.BlockSpec(memory_space=pltpu.VMEM)
    return pl.pallas_call(
        functools.partial(kernel, n),
        out_shape=jax.ShapeDtypeStruct((TOK_DEV, QH * HD), jnp.bfloat16),
        in_specs=[pl.BlockSpec(memory_space=pltpu.HBM)] * 4,
        out_specs=vmem,
        scratch_shapes=[
            pltpu.VMEM(queries.shape, queries.dtype),
            pltpu.VMEM(keys.shape, keys.dtype),
            pltpu.VMEM(values.shape, values.dtype),
            pltpu.VMEM(selected.shape, selected.dtype),
            pltpu.VMEM((n, 2 * KVH, PASS, HD), jnp.bfloat16),
            pltpu.VMEM((PLANE, TOK_DEV, HD), jnp.bfloat16),
            pltpu.VMEM((KVH, rows, HD), jnp.float32),
            pltpu.VMEM((KVH, rows, HD), jnp.float32),
            pltpu.VMEM((KVH, rows, HD), jnp.float32),
            pltpu.SemaphoreType.DMA((n,)),
            pltpu.SemaphoreType.DMA((PLANE,)),
            pltpu.SemaphoreType.DMA((planes, 8)),
            pltpu.SemaphoreType.DMA((8,)),
            pltpu.SemaphoreType.DMA((PLANE,)),
            pltpu.SemaphoreType.DMA((4,)),
        ],
        compiler_params=pltpu.CompilerParams(
            collective_id=0, has_side_effects=True, vmem_limit_bytes=60 * 1024 * 1024),
        cost_estimate=pl.CostEstimate(flops=1300000000, bytes_accessed=4000000, transcendentals=2500000),
    )(queries, keys, values, selected)


def solution(mesh):
    placed = (P("seq", None), P("seq", None), P("seq", None), P("seq", None, None))
    return jax.shard_map(
        functools.partial(body, mesh.shape["seq"]), mesh=mesh, in_specs=placed,
        out_specs=P("seq", None), check_vma=False)
```

```python
import functools
import math

import jax
import jax.numpy as jnp
from jax import lax
from jax.experimental import pallas as pl
from jax.experimental.pallas import tpu as pltpu
from jax.sharding import PartitionSpec as P

HD = 128
QH = 16
KVH = 4
PASS = 32
TOK_DEV = 128
GROUP = QH // KVH
PLANE = 8
LOG2_SCALE = math.log2(math.e) / math.sqrt(HD)
very_negative = -1e30
MESH = pl.DeviceIdType.MESH


def dot_t(a, b):
    return lax.dot_general(a, b, (((1,), (1,)), ((), ())), preferred_element_type=jnp.float32)


def dot(a, b):
    return lax.dot_general(a, b, (((1,), (0,)), ((), ())), preferred_element_type=jnp.float32)


def kernel(n, q_hbm, k_hbm, v_hbm, sel_hbm, o_ref, q_ref, k_ref, v_ref, sel_ref, buf, anchor, acc, best, tot,
           packet_recv, anchor_recv, packet_send, anchor_send, scatter_send, load_sem):
    planes = n // PLANE
    me = lax.axis_index("seq")
    plane = me // PLANE
    r = me % PLANE
    core = r % 2
    x = (r // 2) % 2
    y = r // 4
    near_x = r + 2 - 4 * x
    near_y = r + 4 - 8 * y
    first = near_x * (1 - core) + near_y * core
    second = near_y * (1 - core) + near_x * core
    across = near_x + near_y - r
    to_sib = 1 - 2 * core
    home = plane * PLANE

    barrier = pltpu.get_barrier_semaphore()

    loads = [pltpu.make_async_copy(src, dst, load_sem.at[i]) for i, (src, dst) in enumerate(
        ((sel_hbm, sel_ref), (k_hbm, k_ref), (v_hbm, v_ref), (q_hbm, q_ref)))]
    for load in loads:
        load.start()

    def greet(device):
        pl.semaphore_signal(barrier, inc=1, device_id=(device,), device_id_type=MESH)

    for near in (near_x, near_y, r + to_sib):
        greet(home + near)

    @pl.when(plane > 0)
    def _():
        greet(me - PLANE)

    @pl.when(plane < planes - 1)
    def _():
        greet(me + PLANE)

    is_far = (plane == 0) & (core + x + y >= 2)

    @pl.when(me == 0)
    def _():
        for far in (3, 5, 6, 7):
            greet(far)

    @pl.when(is_far)
    def _():
        greet(0)

    for load in loads[:3]:
        load.wait()

    lane = lax.broadcasted_iota(jnp.int32, (PASS, PASS), 1)
    row = lax.broadcasted_iota(jnp.int32, (PASS, PASS), 0)
    token = lax.broadcasted_iota(jnp.int32, (PASS, TOK_DEV), 1).astype(jnp.float32)
    for g in range(KVH):
        sel = sel_ref[0, g:g + 1, :].astype(jnp.float32)
        column = jnp.sum(jnp.where(lane == row, sel, 0.0), axis=1, keepdims=True)
        one_hot = jnp.where(token == column, 1.0, 0.0).astype(jnp.bfloat16)
        cols = slice(g * HD, (g + 1) * HD)
        buf[me, g] = dot(one_hot, k_ref[:, cols]).astype(jnp.bfloat16)
        buf[me, KVH + g] = dot(one_hot, v_ref[:, cols]).astype(jnp.bfloat16)

    peers = (3 + jnp.where(plane > 0, 1, 0) + jnp.where(plane < planes - 1, 1, 0)
             + jnp.where(me == 0, 4, 0) + jnp.where(is_far, 1, 0))
    pl.semaphore_wait(barrier, peers)

    def remote(ref, send_sem, recv_sem, device):
        return pltpu.make_async_remote_copy(
            src_ref=ref, dst_ref=ref, send_sem=send_sem, recv_sem=recv_sem,
            device_id=(device,), device_id_type=MESH)

    class Stage:
        def __init__(self, piece, recv, send):
            self.piece, self.recv, self.send = piece, recv, send

        def arrived(self, rr):
            remote(self.piece(rr), self.send(0), self.recv(rr), home + first).wait_recv()

        def push(self, rr, target, i):
            remote(self.piece(rr), self.send(i), self.recv(rr), home + target).start()

        def issue(self):
            @pl.when(plane < planes - 1)
            def _():
                remote(self.piece(r), self.send(7), self.recv(r), me + PLANE).start()

            self.push(r, first, 0)
            self.push(r, second, 1)
            self.push(r, r + to_sib, 2)

        def relay(self):
            self.arrived(first)
            self.push(first, second, 3)
            self.push(first, r + to_sib, 4)
            self.arrived(second)
            self.push(second, r + to_sib, 5)

        def finish(self):
            self.arrived(across)
            self.push(across, r + to_sib, 6)

        def gathered(self):
            for rr in (r, first, second, across):
                self.arrived(rr + to_sib)

        def sent(self):
            for i in range(7):
                remote(self.piece(r), self.send(i), self.recv(r), home + first).wait_send()

            @pl.when(plane < planes - 1)
            def _():
                remote(self.piece(r), self.send(7), self.recv(r), me + PLANE).wait_send()

    def packet(q):
        return Stage(lambda rr: buf.at[q * PLANE + rr], lambda rr: packet_recv.at[q * PLANE + rr],
                     lambda i: packet_send.at[q, i])

    block0 = Stage(lambda rr: anchor.at[rr], lambda rr: anchor_recv.at[rr], lambda i: anchor_send.at[i])

    def scatter(j):
        source = k_ref if j < KVH else v_ref
        cols = pl.ds((j % KVH) * HD, HD)
        return pltpu.make_async_remote_copy(
            src_ref=source.at[:, cols], dst_ref=anchor.at[j], send_sem=scatter_send.at[j],
            recv_sem=anchor_recv.at[j], device_id=(j,), device_id_type=MESH)

    @pl.when(me == 0)
    def _():
        for j in range(1, PLANE):
            scatter(j).start()
        anchor[0] = k_ref[:, :HD]

    packet(plane).issue()

    def head_queries(g):
        return jnp.concatenate(
            [q_ref[:, pl.ds(pl.multiple_of((g * GROUP + j) * HD, HD), HD)] for j in range(GROUP)], axis=0)

    def lane_tiles(w):
        return [w[:, i * HD:(i + 1) * HD] for i in range(w.shape[1] // HD)]

    rows = GROUP * TOK_DEV

    def own(g, carry):
        cols = pl.ds(pl.multiple_of(g * HD, HD), HD)
        s = dot_t(head_queries(g), k_ref[:, cols]) * LOG2_SCALE
        position = lax.broadcasted_iota(jnp.int32, (rows, TOK_DEV), 0) % TOK_DEV
        key_at = lax.broadcasted_iota(jnp.int32, (rows, TOK_DEV), 1)
        s = jnp.where(key_at <= position, s, very_negative)
        top = jnp.broadcast_to(jnp.max(s, axis=1, keepdims=True), (rows, HD))
        w = jnp.exp2(s - top)
        best[g] = top
        tot[g] = w
        acc[g] = dot(w.astype(jnp.bfloat16), v_ref[:, cols])
        return carry

    def update(g, key_rows, value_rows, bias):
        s = dot_t(head_queries(g), key_rows) * LOG2_SCALE
        if bias is not None:
            s = s + bias
        tiles = lane_tiles(s)
        old = best[g]
        top = jnp.max(functools.reduce(jnp.maximum, tiles), axis=1, keepdims=True)
        top = jnp.maximum(old, top)
        w = [jnp.exp2(t - top) for t in tiles]
        rescale = jnp.exp2(old - top)
        best[g] = top
        tot[g] = tot[g] * rescale + functools.reduce(jnp.add, w)
        w = jnp.concatenate([t.astype(jnp.bfloat16) for t in w], axis=1)
        acc[g] = acc[g] * rescale + dot(w, value_rows)

    def use_packets(q):
        source = q * PLANE + lax.broadcasted_iota(jnp.int32, (1, PLANE * PASS), 1) // PASS
        bias = jnp.where((source >= 1) & (source < me), 0.0, very_negative)
        at = pl.ds(q * PLANE, PLANE)

        def one(g, carry):
            update(g, buf[at, g].reshape(PLANE * PASS, HD), buf[at, KVH + g].reshape(PLANE * PASS, HD), bias)
            return carry

        lax.fori_loop(0, KVH, one, 0, unroll=True)

    def use_anchor(head):
        for i in range(2):
            update(head + i, anchor[head + i], anchor[KVH + head + i], None)

    loads[3].wait()
    lax.fori_loop(0, KVH, own, 0, unroll=True)

    last = plane + 1

    def step(t, carry):
        def at_stage(s, packets, block):
            @pl.when((s >= 0) & (s <= plane))
            def _():
                packets(plane - s)

            @pl.when(s == last)
            def _():
                block()

        def issue_packets(q):
            packet(q).arrived(r)
            packet(q).issue()

        def issue_block():
            @pl.when(me > 0)
            def _():
                block0.arrived(r)

            block0.issue()

        def compute_packets(q):
            packet(q).gathered()
            use_packets(q)

        def compute_block():
            for rr, other, column in ((r, near_y, x), (near_x, across, 1 - x)):
                block0.arrived(rr + to_sib)
                block0.arrived(other + to_sib)

                @pl.when(me > 0)
                def _():
                    use_anchor(2 * column)

        at_stage(t, issue_packets, issue_block)
        at_stage(t - 1, lambda q: packet(q).relay(), block0.relay)
        at_stage(t - 3, compute_packets, compute_block)
        at_stage(t - 2, lambda q: packet(q).finish(), block0.finish)
        return carry

    lax.fori_loop(1, last + 4, step, 0)

    for g in range(KVH):
        out = acc[g] * (1.0 / jnp.sum(tot[g], axis=1, keepdims=True))
        for j in range(GROUP):
            h = g * GROUP + j
            o_ref[:, h * HD:(h + 1) * HD] = out[j * TOK_DEV:(j + 1) * TOK_DEV].astype(o_ref.dtype)

    def drain(q, carry):
        packet(q).sent()
        return carry

    lax.fori_loop(0, plane + 1, drain, 0)
    block0.sent()

    @pl.when(me == 0)
    def _():
        for j in range(1, PLANE):
            scatter(j).wait_send()


def body(n, queries, keys, values, selected):
    planes = n // PLANE
    rows = GROUP * TOK_DEV
    vmem = pl.BlockSpec(memory_space=pltpu.VMEM)
    return pl.pallas_call(
        functools.partial(kernel, n),
        out_shape=jax.ShapeDtypeStruct((TOK_DEV, QH * HD), jnp.bfloat16),
        in_specs=[pl.BlockSpec(memory_space=pltpu.HBM)] * 4,
        out_specs=vmem,
        scratch_shapes=[
            pltpu.VMEM(queries.shape, queries.dtype),
            pltpu.VMEM(keys.shape, keys.dtype),
            pltpu.VMEM(values.shape, values.dtype),
            pltpu.VMEM(selected.shape, selected.dtype),
            pltpu.VMEM((n, 2 * KVH, PASS, HD), jnp.bfloat16),
            pltpu.VMEM((PLANE, TOK_DEV, HD), jnp.bfloat16),
            pltpu.VMEM((KVH, rows, HD), jnp.float32),
            pltpu.VMEM((KVH, rows, HD), jnp.float32),
            pltpu.VMEM((KVH, rows, HD), jnp.float32),
            pltpu.SemaphoreType.DMA((n,)),
            pltpu.SemaphoreType.DMA((PLANE,)),
            pltpu.SemaphoreType.DMA((planes, 8)),
            pltpu.SemaphoreType.DMA((8,)),
            pltpu.SemaphoreType.DMA((PLANE,)),
            pltpu.SemaphoreType.DMA((4,)),
        ],
        compiler_params=pltpu.CompilerParams(
            collective_id=0, has_side_effects=True, vmem_limit_bytes=60 * 1024 * 1024),
        cost_estimate=pl.CostEstimate(flops=1300000000, bytes_accessed=4000000, transcendentals=2500000),
    )(queries, keys, values, selected)


def solution(mesh):
    placed = (P("seq", None), P("seq", None), P("seq", None), P("seq", None, None))
    return jax.shard_map(
        functools.partial(body, mesh.shape["seq"]), mesh=mesh, in_specs=placed,
        out_specs=P("seq", None), check_vma=False)
```
